32 devices in a mesh: req: 4 (over y, x), kv: 8 (over z, core).
Axes of the slice: x: 2, y: 2, z: 4, core: 2. Of those that a mesh axis runs over, the one named last changes fastest.
Arguments:
- stream: bfloat16 [4096, 2048], P(('req', 'kv')), may hold values from -40 to 40
- projections: bfloat16 [4096, 6144], P(('req', 'kv')), may hold values from -32 to 32
- key_cache: bfloat16 [32768, 2048], P(('req', 'kv')), may hold values from -12 to 12
- value_cache: bfloat16 [32768, 2048], P(('req', 'kv')), may hold values from -6 to 6
- cache_range: int32 [4, 2], replicated, may hold values from 0 to 8192, as said below
- norm_gain: float32 [2048], replicated, may hold values from 0.5 to 1.5
- out_weight: bfloat16 [2048, 2048], P(('req', 'kv')), may hold values from -0.125 to 0.125
- up_weight: bfloat16 [8192, 2048], P(('req', 'kv')), may hold values from -0.125 to 0.125
- down_weight: bfloat16 [8192, 2048], P(('req', 'kv')), may hold values from -0.0625 to 0.0625
Outputs:
- layer_out: bfloat16 [4096, 2048], P(('req', 'kv'))
The draws below stay inside these ranges and needn't reach their ends.
Inputs may be any that keep to these rules, and one draw needn't show every extreme that they name: `cache_range`: row r holds the first and the end of the cached positions that request r attends to: 0 <= first < 2048, first < end <= 8192, and end = 8192 for some request.
All inputs are finite; a program needn't handle non-finite values.
Results may differ from the reference program's by a relative error of at most 0.011.
Values may be sent and summed in bfloat16 or wider, within the bound.
A program may use at most 192 MiB of HBM per device.

```python
import math
import jax
import jax.numpy as jnp
from jax import lax

H = 8
HD = 256
FF = 8192
D = 2048
NEW = 1024
CACHE = 8192
REQS = 4
TOKENS = 4096


def spread_scale(key, shape):
    return jnp.exp(jax.random.uniform(key, shape, jnp.float32, math.log(0.3), math.log(3.0)))


def draw_stream(key, part):
    key_rows, key_cols, key_base = jax.random.split(key, 3)
    row_scale = spread_scale(key_rows, (TOKENS, 1))
    col_scale = spread_scale(key_cols, (1, D))
    base = jax.random.truncated_normal(key_base, -4.0, 4.0, (TOKENS, D), jnp.float32)
    values = base * row_scale * col_scale
    return values.astype(jnp.bfloat16)


def draw_projections(key, part):
    key_base, key_scale = jax.random.split(key, 2)
    base = jax.random.truncated_normal(key_base, -4.0, 4.0, (TOKENS, 3, H, HD), jnp.float32)
    queries = base[:, 0]
    keys = base[:, 1]
    values = base[:, 2]
    scale = spread_scale(key_scale, (TOKENS, H, 1))
    keys = keys * scale
    joined = jnp.stack([queries, keys, values], 1)
    return joined.reshape(TOKENS, 3 * D).astype(jnp.bfloat16)


def draw_key_cache(key, part):
    key_base, key_scale = jax.random.split(key, 2)
    total = REQS * CACHE
    base = jax.random.truncated_normal(key_base, -4.0, 4.0, (total, H, HD), jnp.float32)
    values = base * spread_scale(key_scale, (total, H, 1))
    return values.reshape(total, D).astype(jnp.bfloat16)


def draw_cache_range(key, part):
    key_low, key_span, key_full = jax.random.split(key, 3)
    lower_end = jax.random.randint(key_low, (REQS,), 0, CACHE // 4, jnp.int32)
    extent = CACHE // 8 + jax.random.randint(key_span, (REQS,), 0, CACHE - CACHE // 4 - CACHE // 8 + 1, jnp.int32)
    chosen = jax.random.randint(key_full, (), 0, REQS, jnp.int32)
    upper_end = jnp.where(jnp.arange(REQS, dtype=jnp.int32) == chosen, CACHE, lower_end + extent)
    return jnp.stack([lower_end, upper_end], 1).astype(jnp.int32)


def shard_levels(own_key, dims, cuts, smallest, high):
    level, own = 1.0, jax.random.fold_in(own_key, 6)
    for dim, blocks in cuts:
        draws = jnp.exp(jax.random.uniform(jax.random.fold_in(own, dim), (blocks,), jnp.float32, smallest / len(cuts), high / len(cuts)))
        level = level * jnp.repeat(draws, dims[dim] // blocks).reshape([-1 if axis == dim else 1 for axis in range(len(dims))])
    return level


def normal_values(stream_key, shape, width, reach, pieces=(), kind=jnp.bfloat16):
    drawn = jax.random.normal(stream_key, shape, jnp.float32) * width
    if len(pieces) > 0:
        drawn = shard_levels(stream_key, shape, pieces, -0.22, 0.18) * drawn
    return jnp.clip(drawn, min=-reach, max=reach).astype(kind)


def setup_inputs(seed: int = 0) -> dict:
    seeds = jax.random.split(jax.random.key(seed), 10)
    stream = draw_stream(jax.random.fold_in(seeds[9], 71), 0)
    projections = draw_projections(jax.random.fold_in(seeds[9], 71), 0)
    key_cache = draw_key_cache(jax.random.fold_in(seeds[9], 71), 0)
    value_cache = normal_values(seeds[3], (REQS * CACHE, D), 1.0, 6.0, ((0, 32),))
    cache_range = draw_cache_range(jax.random.fold_in(seeds[9], 71), 0)
    norm_gain = jnp.clip(1.0 + 0.1 * jax.random.normal(seeds[5], (D,), jnp.float32), 0.5, 1.5)
    out_weight = normal_values(seeds[6], (D, D), D ** -0.5, 0.125, ((0, 32),))
    up_weight = normal_values(seeds[7], (FF, D), D ** -0.5, 0.125, ((0, 32),))
    down_weight = normal_values(seeds[8], (FF, D), FF ** -0.5, 0.0625, ((0, 32),))
    return {"stream": stream, "projections": projections, "key_cache": key_cache, "value_cache": value_cache, "cache_range": cache_range, "norm_gain": norm_gain, "out_weight": out_weight, "up_weight": up_weight, "down_weight": down_weight}


def layer_norm(stream, norm_gain):
    values = stream.astype(jnp.float32)
    centred = values - lax.optimization_barrier(jnp.mean(values, axis=-1, keepdims=True))
    spread = lax.optimization_barrier(jnp.mean(centred * centred, axis=-1, keepdims=True))
    return centred * lax.rsqrt(spread + 1e-05) * norm_gain

def reference(stream, projections, key_cache, value_cache, cache_range, norm_gain, out_weight, up_weight, down_weight):
    score_scale = 1.0 / math.sqrt(HD)

    def one_request(index):
        index = index.astype(jnp.int32)
        rows = lax.dynamic_slice_in_dim(projections, index * NEW, NEW, 0)
        queries = rows[:, :D].astype(jnp.float32).reshape(NEW, H, HD)
        new_keys = rows[:, D:2 * D].astype(jnp.float32).reshape(NEW, H, HD)
        new_values = rows[:, 2 * D:].astype(jnp.float32).reshape(NEW, H, HD)
        cached_keys = lax.dynamic_slice_in_dim(key_cache, index * CACHE, CACHE, 0).astype(jnp.float32).reshape(CACHE, H, HD)
        cached_values = lax.dynamic_slice_in_dim(value_cache, index * CACHE, CACHE, 0).astype(jnp.float32).reshape(CACHE, H, HD)
        key_rows = jnp.concatenate([cached_keys, new_keys], 0)
        value_rows = jnp.concatenate([cached_values, new_values], 0)
        lower_end = cache_range[index, 0]
        upper_end = cache_range[index, 1]
        positions = jnp.arange(CACHE, dtype=jnp.int32)
        cache_visible = (positions >= lower_end) & (positions < upper_end)
        token_pos = jnp.arange(NEW, dtype=jnp.int32)
        new_visible = token_pos[None, :] <= token_pos[:, None]
        visible = jnp.concatenate([jnp.broadcast_to(cache_visible[None, :], (NEW, CACHE)), new_visible], 1)
        scores = jnp.einsum('qhd,khd->hqk', queries, key_rows) * score_scale
        scores = jnp.where(visible[None], scores, -1e+30)
        row_max = lax.optimization_barrier(jnp.max(scores, axis=-1, keepdims=True))
        weights = jnp.where(visible[None], jnp.exp(scores - row_max), 0.0)
        denominator = lax.optimization_barrier(jnp.sum(weights, axis=-1))
        rounded = lax.optimization_barrier(weights.astype(jnp.bfloat16)).astype(jnp.float32)
        numerator = jnp.einsum('hqk,khd->qhd', rounded, value_rows)
        attention = (numerator / jnp.transpose(denominator)[..., None]).reshape(NEW, D).astype(jnp.bfloat16)
        stream_rows = lax.dynamic_slice_in_dim(stream, index * NEW, NEW, 0)
        normed = layer_norm(stream_rows, norm_gain).astype(jnp.bfloat16)
        gates = lax.dot_general(normed, up_weight, (((1,), (1,)), ((), ())), preferred_element_type=jnp.float32)
        hidden = jax.nn.gelu(gates, approximate=False).astype(jnp.bfloat16)
        summed = jnp.dot(attention, out_weight, preferred_element_type=jnp.float32) + jnp.dot(hidden, down_weight, preferred_element_type=jnp.float32)
        return (stream_rows.astype(jnp.float32) + summed).astype(jnp.bfloat16)
    results = lax.map(one_request, jnp.arange(REQS, dtype=jnp.int32))
    return results.reshape(TOKENS, D)
```

```python
import jax
import jax.numpy as jnp
from jax import lax
from jax.experimental import pallas as pl
from jax.experimental.pallas import tpu as pltpu
from jax.sharding import PartitionSpec as P

HD = 256
SPAN = 8
CORES = 2
CHIPS = SPAN // CORES
LOWEST = -1e29
NEG_FILL = -1e30
NORM_EPS = 1e-05
ROW_TILE = 256
F32 = jnp.float32
BF16 = jnp.bfloat16


def swap_cores(value):
    pairs = [(k, k ^ 1) for k in range(lax.axis_size("kv"))]
    return lax.ppermute(value, "kv", pairs)


def next_chip(value):
    pairs = [
        (k, k - k % SPAN + (k % SPAN + CORES) % SPAN) for k in range(lax.axis_size("kv"))
    ]
    return lax.ppermute(value, "kv", pairs)


def gather_chips(value):
    size = lax.axis_size("kv")
    groups = [
        [first + core + CORES * chip for chip in range(CHIPS)]
        for first in range(0, size, SPAN)
        for core in range(CORES)
    ]
    return lax.all_gather(value, "kv", axis=0, tiled=True, axis_index_groups=groups)


def gather_requests(value):
    size = lax.axis_size("kv")
    if size > SPAN:
        groups = [list(range(m, size, SPAN)) for m in range(SPAN)]
        value = lax.all_gather(value, "kv", axis=0, tiled=True, axis_index_groups=groups)
    return lax.all_gather(value, "req", axis=0, tiled=True)


def layer_norm(stream, norm_gain):
    values = stream.astype(F32)
    centred = values - jnp.mean(values, axis=-1, keepdims=True)
    spread = jnp.mean(centred * centred, axis=-1, keepdims=True)
    return (centred * lax.rsqrt(spread + NORM_EPS) * norm_gain).astype(BF16)


def attend_kernel(
    meta, q_mine, q_other, key, value, new_key, new_value, bias, out, lse, value_t, new_value_t
):
    slot = pl.program_id(0)
    core = meta[2]
    member = meta[3]
    half = q_mine.shape[0]
    token_count = new_key.shape[0]
    value_t[...] = value[...].T
    new_value_t[...] = new_value[...].T
    for first in (0, 1):
        source = q_mine if first == 0 else q_other
        source_core = core if first == 0 else 1 - core
        place = jnp.where(slot == 0, first, 1 - first) * half
        for tile in range(half // ROW_TILE):
            queries = source[pl.ds(tile * ROW_TILE, ROW_TILE), :] * BF16(1.0 / 16.0)
            scores = lax.dot_general(
                key[...], queries, (((1,), (1,)), ((), ())), preferred_element_type=F32
            )
            scores = scores + bias[...]
            fresh = lax.dot_general(
                new_key[...], queries, (((1,), (1,)), ((), ())), preferred_element_type=F32
            )
            row = tile * ROW_TILE + lax.broadcasted_iota(jnp.int32, (1, ROW_TILE), 1)
            chip = row // token_count
            token = row + chip * token_count + source_core * token_count
            position = member * token_count + lax.broadcasted_iota(
                jnp.int32, (token_count, 1), 0
            )
            fresh = jnp.where(position <= token, fresh, NEG_FILL)
            largest = jnp.maximum(
                jnp.max(scores, axis=0, keepdims=True), jnp.max(fresh, axis=0, keepdims=True)
            )
            largest = jnp.maximum(largest, LOWEST)
            weights = jnp.exp(scores - largest)
            fresh = jnp.exp(fresh - largest)
            total = jnp.sum(weights, axis=0, keepdims=True) + jnp.sum(
                fresh, axis=0, keepdims=True
            )
            total = jnp.maximum(total, 1.0)
            sums = jnp.dot(
                value_t[...], weights.astype(BF16), preferred_element_type=F32
            ) + jnp.dot(new_value_t[...], fresh.astype(BF16), preferred_element_type=F32)
            lanes = pl.ds(pl.multiple_of(place + tile * ROW_TILE, ROW_TILE), ROW_TILE)
            out[0, :, lanes] = (sums / total).astype(BF16)
            lse[0, :, lanes] = largest + jnp.log(total)


def attend(meta, q_mine, q_other, key_cache, value_cache, projections, bias):
    half = q_mine.shape[0]
    cache_rows = key_cache.shape[0]
    token_count = projections.shape[0]
    heads = key_cache.shape[1] // HD
    q_spec = pl.BlockSpec((half, HD), lambda i, meta: (0, meta[i]))
    cache_spec = pl.BlockSpec((cache_rows, HD), lambda i, meta: (0, meta[i]))
    flops = 2 * 2 * 2 * 2 * half * (cache_rows + token_count) * HD
    return pl.pallas_call(
        attend_kernel,
        grid_spec=pltpu.PrefetchScalarGridSpec(
            num_scalar_prefetch=1,
            grid=(CORES,),
            in_specs=[
                q_spec,
                q_spec,
                cache_spec,
                cache_spec,
                pl.BlockSpec((token_count, HD), lambda i, meta: (0, heads + meta[i])),
                pl.BlockSpec((token_count, HD), lambda i, meta: (0, 2 * heads + meta[i])),
                pl.BlockSpec((cache_rows, 1), lambda i, meta: (0, 0)),
            ],
            out_specs=[
                pl.BlockSpec((1, HD, 2 * half), lambda i, meta: (i, 0, 0)),
                pl.BlockSpec((1, 1, 2 * half), lambda i, meta: (i, 0, 0)),
            ],
            scratch_shapes=[
                pltpu.VMEM((HD, cache_rows), BF16),
                pltpu.VMEM((HD, token_count), BF16),
            ],
        ),
        out_shape=[
            jax.ShapeDtypeStruct((CORES, HD, 2 * half), BF16),
            jax.ShapeDtypeStruct((CORES, 1, 2 * half), F32),
        ],
        compiler_params=pltpu.CompilerParams(vmem_limit_bytes=40 * 2**20),
        cost_estimate=pl.CostEstimate(
            flops=flops, bytes_accessed=8 * 2**20, transcendentals=flops // (4 * HD)
        ),
    )(meta, q_mine, q_other, key_cache, value_cache, projections, projections, bias)


def merge(parts):
    largest = parts[0][1]
    for part in parts[1:]:
        largest = jnp.maximum(largest, part[1])
    shares = [jnp.exp(part[1] - largest) for part in parts]
    total = sum(shares)
    joined = sum(part[0].astype(F32) * (share / total) for part, share in zip(parts, shares))
    return joined.astype(BF16), largest + jnp.log(total)


def on_device(
    stream,
    projections,
    key_cache,
    value_cache,
    cache_range,
    norm_gain,
    out_weight,
    up_weight,
    down_weight,
):
    token_count, width = stream.shape
    cache_rows = key_cache.shape[0]
    kv_count = lax.axis_size("kv")
    device_count = kv_count * lax.axis_size("req")
    request_count = device_count // SPAN
    kv_place = lax.axis_index("kv")
    member = kv_place % SPAN
    core = member % CORES
    chip = member // CORES
    request = (lax.axis_index("req") * kv_count + kv_place) // SPAN

    q_mine = gather_chips(projections[:, :width])
    q_other = swap_cores(q_mine)
    up_rows = gather_requests(up_weight)
    down_rows = gather_requests(down_weight)
    head_pairs = [
        (d, (d % request_count) * SPAN + d // request_count) for d in range(device_count)
    ]
    out_rows = gather_requests(lax.ppermute(out_weight, ("req", "kv"), head_pairs))

    bounds = lax.dynamic_slice_in_dim(cache_range, request, 1, 0)[0]
    positions = member * cache_rows + jnp.arange(cache_rows, dtype=jnp.int32)[:, None]
    bias = jnp.where((positions >= bounds[0]) & (positions < bounds[1]), 0.0, NEG_FILL)
    bias = bias.astype(F32)

    normed, _ = lax.optimization_barrier((layer_norm(stream, norm_gain), q_mine))
    rows_mine = gather_chips(normed)
    rows_other = swap_cores(rows_mine)

    carried = None
    for phase in range(CHIPS):
        target = (chip + CHIPS - 1 - phase) % CHIPS
        kept = CORES * target + core
        given = CORES * target + 1 - core
        meta = jnp.stack([kept, given, core, member]).astype(jnp.int32)
        out, lse = attend(meta, q_mine, q_other, key_cache, value_cache, projections, bias)
        parts = [(out[0], lse[0]), swap_cores((out[1], lse[1]))]
        if carried is not None:
            parts.append(carried)
        carried = merge(parts)
        if phase < CHIPS - 1:
            carried = next_chip(carried)
    attention = carried[0]

    def hidden_of(rows):
        gates = lax.dot_general(
            rows, up_rows, (((1,), (1,)), ((), ())), preferred_element_type=F32
        )
        return jax.nn.gelu(gates, approximate=False).astype(BF16)

    hidden_mine = hidden_of(rows_mine)
    hidden_other = hidden_of(rows_other)
    half = CHIPS * token_count
    running = None
    for phase in range(CHIPS):
        first = ((chip + CHIPS - 1 - phase) % CHIPS) * token_count

        def share(hidden, offset):
            block = lax.dynamic_slice_in_dim(attention, offset + first, token_count, 1)
            branch = lax.dot_general(
                block, out_rows, (((0,), (0,)), ((), ())), preferred_element_type=F32
            )
            units = lax.dynamic_slice_in_dim(hidden, first, token_count, 0)
            return branch + jnp.dot(units, down_rows, preferred_element_type=F32)

        total = share(hidden_mine, 0)
        total = total + swap_cores(share(hidden_other, half).astype(BF16)).astype(F32)
        if running is not None:
            total = total + running.astype(F32)
        running = total
        if phase < CHIPS - 1:
            running = next_chip(total.astype(BF16))
    return (stream.astype(F32) + running).astype(BF16)


def solution(mesh):
    rows = P(("req", "kv"), None)
    in_specs = (rows, rows, rows, rows, P(), P(), rows, rows, rows)
    return jax.shard_map(
        on_device, mesh=mesh, in_specs=in_specs, out_specs=rows, check_vma=False
    )
```

```python
import jax
import jax.numpy as jnp
from jax import lax
from jax.experimental import pallas as pl
from jax.experimental.pallas import tpu as pltpu
from jax.sharding import PartitionSpec as P

HD = 256
SPAN = 8
CORES = 2
CHIPS = SPAN // CORES
LOWEST = -1e29
NEG_FILL = -1e30
NORM_EPS = 1e-05
F32 = jnp.float32
BF16 = jnp.bfloat16


def swap_cores(value):
    pairs = [(k, k ^ 1) for k in range(lax.axis_size("kv"))]
    return lax.ppermute(value, "kv", pairs)


def next_chip(value):
    pairs = [
        (k, k - k % SPAN + (k % SPAN + CORES) % SPAN) for k in range(lax.axis_size("kv"))
    ]
    return lax.ppermute(value, "kv", pairs)


def gather_ring(value):
    pieces = [value]
    for _ in range(CHIPS - 1):
        pieces.append(next_chip(pieces[-1]))
    return pieces, [swap_cores(piece) for piece in pieces]


def gather_requests(value, low_first):
    device_count = lax.axis_size("kv") * lax.axis_size("req")
    bits = range((device_count // SPAN).bit_length() - 1)
    pieces = {0: value}
    for bit in bits if low_first else reversed(bits):
        pairs = [(d, d ^ (SPAN << bit)) for d in range(device_count)]
        for index in list(pieces):
            pieces[index | 1 << bit] = lax.ppermute(pieces[index], ("req", "kv"), pairs)
    return [pieces[index] for index in range(len(pieces))]


def gather_in_order(value):
    size = lax.axis_size("kv")
    if size > SPAN:
        groups = [list(range(m, size, SPAN)) for m in range(SPAN)]
        value = lax.all_gather(value, "kv", axis=0, tiled=True, axis_index_groups=groups)
    return lax.all_gather(value, "req", axis=0, tiled=True)


def layer_norm(stream, norm_gain):
    values = stream.astype(F32)
    centred = values - jnp.mean(values, axis=-1, keepdims=True)
    spread = jnp.mean(centred * centred, axis=-1, keepdims=True)
    return (centred * lax.rsqrt(spread + NORM_EPS) * norm_gain).astype(BF16)


def attend_kernel(meta, *refs):
    pieces = refs[: 2 * CHIPS]
    key, value, new_key, new_value, bias, out, lse, value_t, new_value_t = refs[2 * CHIPS :]
    slot = pl.program_id(0)
    core = meta[2]
    member = meta[3]
    chip = member // CORES
    token_count = new_key.shape[0]
    half = CHIPS * token_count
    value_t[...] = value[...].T
    new_value_t[...] = new_value[...].T
    position = member * token_count + lax.broadcasted_iota(jnp.int32, (token_count, 1), 0)
    lane = lax.broadcasted_iota(jnp.int32, (1, token_count), 1)
    for first in (0, 1):
        source_core = core if first == 0 else 1 - core
        place = jnp.where(slot == 0, first, 1 - first) * half
        for pair in range(0, CHIPS, 2):
            steps = (pair, pair + 1)
            chips = [lax.rem(chip - step + CHIPS, CHIPS) for step in steps]
            queries = jnp.concatenate(
                [pieces[first * CHIPS + step][...] for step in steps], 0
            ) * BF16(HD**-0.5)
            scores = lax.dot_general(
                key[...], queries, (((1,), (1,)), ((), ())), preferred_element_type=F32
            )
            scores = scores + bias[...]
            fresh = lax.dot_general(
                new_key[...], queries, (((1,), (1,)), ((), ())), preferred_element_type=F32
            )
            token = jnp.concatenate(
                [(CORES * place_z + source_core) * token_count + lane for place_z in chips], 1
            )
            fresh = jnp.where(position <= token, fresh, NEG_FILL)
            largest = jnp.maximum(
                jnp.max(scores, axis=0, keepdims=True), jnp.max(fresh, axis=0, keepdims=True)
            )
            largest = jnp.maximum(largest, LOWEST)
            weights = jnp.exp(scores - largest)
            fresh = jnp.exp(fresh - largest)
            total = jnp.sum(weights, axis=0, keepdims=True) + jnp.sum(
                fresh, axis=0, keepdims=True
            )
            total = jnp.maximum(total, 1.0)
            sums = jnp.dot(
                value_t[...], weights.astype(BF16), preferred_element_type=F32
            ) + jnp.dot(new_value_t[...], fresh.astype(BF16), preferred_element_type=F32)
            sums = (sums / total).astype(BF16)
            logs = largest + jnp.log(total)
            for step, place_z in enumerate(chips):
                lanes = pl.ds(
                    pl.multiple_of(place + place_z * token_count, token_count), token_count
                )
                held = slice(step * token_count, (step + 1) * token_count)
                out[0, :, lanes] = sums[:, held]
                lse[0, :, lanes] = logs[:, held]


def attend(meta, pieces, key_cache, value_cache, projections, bias):
    token_count = projections.shape[0]
    new_total = len(pieces) * token_count
    cache_rows = key_cache.shape[0]
    heads = key_cache.shape[1] // HD
    q_spec = pl.BlockSpec((token_count, HD), lambda i, meta: (0, meta[i]))
    cache_spec = pl.BlockSpec((cache_rows, HD), lambda i, meta: (0, meta[i]))
    flops = 2 * 2 * CORES * new_total * (cache_rows + token_count) * HD
    return pl.pallas_call(
        attend_kernel,
        grid_spec=pltpu.PrefetchScalarGridSpec(
            num_scalar_prefetch=1,
            grid=(CORES,),
            in_specs=[q_spec] * len(pieces)
            + [
                cache_spec,
                cache_spec,
                pl.BlockSpec((token_count, HD), lambda i, meta: (0, heads + meta[i])),
                pl.BlockSpec((token_count, HD), lambda i, meta: (0, 2 * heads + meta[i])),
                pl.BlockSpec((cache_rows, 1), lambda i, meta: (0, 0)),
            ],
            out_specs=[
                pl.BlockSpec((1, HD, new_total), lambda i, meta: (i, 0, 0)),
                pl.BlockSpec((1, 1, new_total), lambda i, meta: (i, 0, 0)),
            ],
            scratch_shapes=[
                pltpu.VMEM((HD, cache_rows), BF16),
                pltpu.VMEM((HD, token_count), BF16),
            ],
        ),
        out_shape=[
            jax.ShapeDtypeStruct((CORES, HD, new_total), BF16),
            jax.ShapeDtypeStruct((CORES, 1, new_total), F32),
        ],
        compiler_params=pltpu.CompilerParams(vmem_limit_bytes=40 * 2**20),
        cost_estimate=pl.CostEstimate(
            flops=flops, bytes_accessed=8 * 2**20, transcendentals=flops // (4 * HD)
        ),
    )(meta, *pieces, key_cache, value_cache, projections, projections, bias)


def merge(parts):
    largest = parts[0][1]
    for part in parts[1:]:
        largest = jnp.maximum(largest, part[1])
    shares = [jnp.exp(part[1] - largest) for part in parts]
    total = sum(shares)
    joined = sum(part[0].astype(F32) * (share / total) for part, share in zip(parts, shares))
    return joined.astype(BF16), largest + jnp.log(total)


def on_device(
    stream,
    projections,
    key_cache,
    value_cache,
    cache_range,
    norm_gain,
    out_weight,
    up_weight,
    down_weight,
):
    token_count, width = stream.shape
    cache_rows = key_cache.shape[0]
    kv_count = lax.axis_size("kv")
    device_count = kv_count * lax.axis_size("req")
    request_count = device_count // SPAN
    kv_place = lax.axis_index("kv")
    member = kv_place % SPAN
    core = member % CORES
    chip = member // CORES
    request = (lax.axis_index("req") * kv_count + kv_place) // SPAN

    q_mine, q_other = gather_ring(projections[:, :width])
    up_rows = jnp.concatenate(gather_requests(up_weight, True), 0)
    down_rows = jnp.concatenate(gather_requests(down_weight, False), 0)
    head_pairs = [
        (d, (d % request_count) * SPAN + d // request_count) for d in range(device_count)
    ]
    out_rows = gather_in_order(lax.ppermute(out_weight, ("req", "kv"), head_pairs))

    bounds = lax.dynamic_slice_in_dim(cache_range, request, 1, 0)[0]
    positions = member * cache_rows + jnp.arange(cache_rows, dtype=jnp.int32)[:, None]
    bias = jnp.where((positions >= bounds[0]) & (positions < bounds[1]), 0.0, NEG_FILL)
    bias = bias.astype(F32)

    normed, _ = lax.optimization_barrier((layer_norm(stream, norm_gain), q_mine[-1]))
    rows_mine, rows_other = gather_ring(normed)

    carried = None
    for phase in range(CHIPS):
        target = (chip + CHIPS - 1 - phase) % CHIPS
        kept = CORES * target + core
        given = CORES * target + 1 - core
        meta = jnp.stack([kept, given, core, member]).astype(jnp.int32)
        out, lse = attend(meta, q_mine + q_other, key_cache, value_cache, projections, bias)
        parts = [(out[0], lse[0]), swap_cores((out[1], lse[1]))]
        if carried is not None:
            parts.append(carried)
        carried = merge(parts)
        if phase < CHIPS - 1:
            carried = next_chip(carried)
    attention = carried[0]

    gates = lax.dot_general(
        jnp.concatenate(rows_mine + rows_other, 0),
        up_rows,
        (((1,), (1,)), ((), ())),
        preferred_element_type=F32,
    )
    hidden = jax.nn.gelu(gates, approximate=False).astype(BF16)
    units = jnp.dot(hidden, down_rows, preferred_element_type=F32)
    half = CHIPS * token_count
    running = None
    for phase in range(CHIPS):
        step = (phase + 1) % CHIPS
        first = ((chip + CHIPS - step) % CHIPS) * token_count

        def share(offset):
            block = lax.dynamic_slice_in_dim(attention, offset + first, token_count, 1)
            branch = lax.dot_general(
                block, out_rows, (((0,), (0,)), ((), ())), preferred_element_type=F32
            )
            held = offset + step * token_count
            return branch + units[held : held + token_count]

        total = share(0) + swap_cores(share(half).astype(BF16)).astype(F32)
        if running is not None:
            total = total + running.astype(F32)
        running = total
        if phase < CHIPS - 1:
            running = next_chip(total.astype(BF16))
    return (stream.astype(F32) + running).astype(BF16)


def solution(mesh):
    rows = P(("req", "kv"), None)
    in_specs = (rows, rows, rows, rows, P(), P(), rows, rows, rows)
    return jax.shard_map(
        on_device, mesh=mesh, in_specs=in_specs, out_specs=rows, check_vma=False
    )
```

```python
import jax
import jax.numpy as jnp
from jax import lax
from jax.experimental import pallas as pl
from jax.experimental.pallas import tpu as pltpu
from jax.sharding import PartitionSpec as P

HD = 256
SPAN = 8
CORES = 2
CHIPS = SPAN // CORES
LOWEST = -1e29
NEG_FILL = -1e30
NORM_EPS = 1e-05
F32 = jnp.float32
BF16 = jnp.bfloat16


def swap_cores(value):
    pairs = [(k, k ^ 1) for k in range(lax.axis_size("kv"))]
    return lax.ppermute(value, "kv", pairs)


def next_chip(value):
    pairs = [
        (k, k - k % SPAN + (k % SPAN + CORES) % SPAN) for k in range(lax.axis_size("kv"))
    ]
    return lax.ppermute(value, "kv", pairs)


def gather_ring(value):
    pieces = [value]
    for _ in range(CHIPS - 1):
        pieces.append(next_chip(pieces[-1]))
    return pieces


def widen(pieces, bit):
    device_count = lax.axis_size("kv") * lax.axis_size("req")
    pairs = [(d, d ^ (SPAN << bit)) for d in range(device_count)]
    found = dict(pieces)
    for index, piece in pieces.items():
        found[index | 1 << bit] = lax.ppermute(piece, ("req", "kv"), pairs)
    return found


def gather_in_order(value):
    size = lax.axis_size("kv")
    if size > SPAN:
        groups = [list(range(m, size, SPAN)) for m in range(SPAN)]
        value = lax.all_gather(value, "kv", axis=0, tiled=True, axis_index_groups=groups)
    return lax.all_gather(value, "req", axis=0, tiled=True)


def layer_norm(stream, norm_gain):
    values = stream.astype(F32)
    centred = values - jnp.mean(values, axis=-1, keepdims=True)
    spread = jnp.mean(centred * centred, axis=-1, keepdims=True)
    return (centred * lax.rsqrt(spread + NORM_EPS) * norm_gain).astype(BF16)


def attend_kernel(meta, *refs):
    pieces = refs[: 2 * CHIPS]
    key, value, new_key, new_value, bias, out, lse, value_t, new_value_t = refs[2 * CHIPS :]
    slot = pl.program_id(0)
    core = meta[2]
    member = meta[3]
    chip = member // CORES
    token_count = new_key.shape[0]
    half = CHIPS * token_count
    value_t[...] = value[...].T
    new_value_t[...] = new_value[...].T
    position = member * token_count + lax.broadcasted_iota(jnp.int32, (token_count, 1), 0)
    lane = lax.broadcasted_iota(jnp.int32, (1, token_count), 1)
    for first in (0, 1):
        source_core = core if first == 0 else 1 - core
        place = jnp.where(slot == 0, first, 1 - first) * half
        for pair in range(0, CHIPS, 2):
            steps = (pair, pair + 1)
            chips = [lax.rem(chip - step + CHIPS, CHIPS) for step in steps]
            queries = jnp.concatenate(
                [pieces[first * CHIPS + step][...] for step in steps], 0
            ) * BF16(HD**-0.5)
            scores = lax.dot_general(
                key[...], queries, (((1,), (1,)), ((), ())), preferred_element_type=F32
            )
            scores = scores + bias[...]
            fresh = lax.dot_general(
                new_key[...], queries, (((1,), (1,)), ((), ())), preferred_element_type=F32
            )
            token = jnp.concatenate(
                [(CORES * place_z + source_core) * token_count + lane for place_z in chips], 1
            )
            fresh = jnp.where(position <= token, fresh, NEG_FILL)
            largest = jnp.maximum(
                jnp.max(scores, axis=0, keepdims=True), jnp.max(fresh, axis=0, keepdims=True)
            )
            largest = jnp.maximum(largest, LOWEST)
            weights = jnp.exp(scores - largest)
            fresh = jnp.exp(fresh - largest)
            total = jnp.sum(weights, axis=0, keepdims=True) + jnp.sum(
                fresh, axis=0, keepdims=True
            )
            total = jnp.maximum(total, 1.0)
            sums = jnp.dot(
                value_t[...], weights.astype(BF16), preferred_element_type=F32
            ) + jnp.dot(new_value_t[...], fresh.astype(BF16), preferred_element_type=F32)
            sums = (sums / total).astype(BF16)
            logs = largest + jnp.log(total)
            for step, place_z in enumerate(chips):
                lanes = pl.ds(
                    pl.multiple_of(place + place_z * token_count, token_count), token_count
                )
                held = slice(step * token_count, (step + 1) * token_count)
                out[0, :, lanes] = sums[:, held]
                lse[0, :, lanes] = logs[:, held]


def attend(meta, pieces, key_cache, value_cache, projections, bias):
    token_count = projections.shape[0]
    new_total = len(pieces) * token_count
    cache_rows = key_cache.shape[0]
    heads = key_cache.shape[1] // HD
    q_spec = pl.BlockSpec((token_count, HD), lambda i, meta: (0, meta[i]))
    cache_spec = pl.BlockSpec((cache_rows, HD), lambda i, meta: (0, meta[i]))
    flops = 2 * 2 * CORES * new_total * (cache_rows + token_count) * HD
    return pl.pallas_call(
        attend_kernel,
        grid_spec=pltpu.PrefetchScalarGridSpec(
            num_scalar_prefetch=1,
            grid=(CORES,),
            in_specs=[q_spec] * len(pieces)
            + [
                cache_spec,
                cache_spec,
                pl.BlockSpec((token_count, HD), lambda i, meta: (0, heads + meta[i])),
                pl.BlockSpec((token_count, HD), lambda i, meta: (0, 2 * heads + meta[i])),
                pl.BlockSpec((cache_rows, 1), lambda i, meta: (0, 0)),
            ],
            out_specs=[
                pl.BlockSpec((1, HD, new_total), lambda i, meta: (i, 0, 0)),
                pl.BlockSpec((1, 1, new_total), lambda i, meta: (i, 0, 0)),
            ],
            scratch_shapes=[
                pltpu.VMEM((HD, cache_rows), BF16),
                pltpu.VMEM((HD, token_count), BF16),
            ],
        ),
        out_shape=[
            jax.ShapeDtypeStruct((CORES, HD, new_total), BF16),
            jax.ShapeDtypeStruct((CORES, 1, new_total), F32),
        ],
        compiler_params=pltpu.CompilerParams(vmem_limit_bytes=40 * 2**20),
        cost_estimate=pl.CostEstimate(
            flops=flops, bytes_accessed=8 * 2**20, transcendentals=flops // (4 * HD)
        ),
    )(meta, *pieces, key_cache, value_cache, projections, projections, bias)


def merge(parts):
    largest = parts[0][1]
    for part in parts[1:]:
        largest = jnp.maximum(largest, part[1])
    shares = [jnp.exp(part[1] - largest) for part in parts]
    total = sum(shares)
    joined = sum(part[0].astype(F32) * (share / total) for part, share in zip(parts, shares))
    return joined.astype(BF16), largest + jnp.log(total)


def on_device(
    stream,
    projections,
    key_cache,
    value_cache,
    cache_range,
    norm_gain,
    out_weight,
    up_weight,
    down_weight,
):
    token_count, width = stream.shape
    cache_rows = key_cache.shape[0]
    kv_count = lax.axis_size("kv")
    device_count = kv_count * lax.axis_size("req")
    request_count = device_count // SPAN
    kv_place = lax.axis_index("kv")
    member = kv_place % SPAN
    core = member % CORES
    chip = member // CORES
    request = (lax.axis_index("req") * kv_count + kv_place) // SPAN

    bits = list(range(request_count.bit_length() - 1))
    q_mine = [projections[:, :width]]
    up_pieces, down_pieces = {0: up_weight}, {0: down_weight}
    for step in range(CHIPS - 2):
        q_mine.append(next_chip(q_mine[-1]))
    up_pieces = widen(up_pieces, bits[0])
    down_pieces = widen(down_pieces, bits[-1])
    q_mine[-1], up_pieces, down_pieces = lax.optimization_barrier(
        (q_mine[-1], up_pieces, down_pieces)
    )
    q_mine.append(next_chip(q_mine[-1]))
    q_other = [swap_cores(piece) for piece in q_mine]
    for bit in bits[1:]:
        up_pieces = widen(up_pieces, bit)
    for bit in reversed(bits[:-1]):
        down_pieces = widen(down_pieces, bit)
    head_pairs = [
        (d, (d % request_count) * SPAN + d // request_count) for d in range(device_count)
    ]
    out_rows = gather_in_order(lax.ppermute(out_weight, ("req", "kv"), head_pairs))

    bounds = lax.dynamic_slice_in_dim(cache_range, request, 1, 0)[0]
    positions = member * cache_rows + jnp.arange(cache_rows, dtype=jnp.int32)[:, None]
    bias = jnp.where((positions >= bounds[0]) & (positions < bounds[1]), 0.0, NEG_FILL)
    bias = bias.astype(F32)

    normed, _ = lax.optimization_barrier((layer_norm(stream, norm_gain), q_mine[-1]))
    rows_mine = gather_ring(normed)
    rows_other = [swap_cores(piece) for piece in rows_mine]

    carried = None
    for phase in range(CHIPS):
        target = (chip + CHIPS - 1 - phase) % CHIPS
        kept = CORES * target + core
        given = CORES * target + 1 - core
        meta = jnp.stack([kept, given, core, member]).astype(jnp.int32)
        if phase == CHIPS - 1:
            meta, up_pieces, down_pieces = lax.optimization_barrier(
                (meta, up_pieces, down_pieces)
            )
        out, lse = attend(meta, q_mine + q_other, key_cache, value_cache, projections, bias)
        parts = [(out[0], lse[0]), swap_cores((out[1], lse[1]))]
        if carried is not None:
            parts.append(carried)
        carried = merge(parts)
        if phase < CHIPS - 1:
            carried = next_chip(carried)
    up_rows = jnp.concatenate([up_pieces[i] for i in range(request_count)], 0)
    down_rows = jnp.concatenate([down_pieces[i] for i in range(request_count)], 0)
    units = []
    for step in range(CHIPS):
        gates = lax.dot_general(
            jnp.concatenate([rows_mine[step], rows_other[step]], 0),
            up_rows,
            (((1,), (1,)), ((), ())),
            preferred_element_type=F32,
        )
        hidden = jax.nn.gelu(gates, approximate=False).astype(BF16)
        units.append(jnp.dot(hidden, down_rows, preferred_element_type=F32))
    attention, units = lax.optimization_barrier((carried[0], units))

    half = CHIPS * token_count
    order = [(step + 1) % CHIPS for step in range(CHIPS)]
    firsts = [((chip + CHIPS - step) % CHIPS) * token_count for step in order]

    def branch(offset):
        block = jnp.concatenate(
            [
                lax.dynamic_slice_in_dim(attention, offset + first, token_count, 1)
                for first in firsts
            ],
            1,
        )
        return lax.dot_general(
            block, out_rows, (((0,), (0,)), ((), ())), preferred_element_type=F32
        )

    given, kept = branch(half), branch(0)
    received = []
    for phase, step in enumerate(order):
        rows = slice(phase * token_count, (phase + 1) * token_count)
        received.append(swap_cores((given[rows] + units[step][token_count:]).astype(BF16)))
    running = None
    for phase, step in enumerate(order):
        rows = slice(phase * token_count, (phase + 1) * token_count)
        total = kept[rows] + units[step][:token_count] + received[phase].astype(F32)
        if running is not None:
            total = total + running.astype(F32)
        running = total
        if phase < CHIPS - 1:
            running = next_chip(total.astype(BF16))
    return (stream.astype(F32) + running).astype(BF16)


def solution(mesh):
    rows = P(("req", "kv"), None)
    in_specs = (rows, rows, rows, rows, P(), P(), rows, rows, rows)
    return jax.shard_map(
        on_device, mesh=mesh, in_specs=in_specs, out_specs=rows, check_vma=False
    )
```

```python
import jax
import jax.numpy as jnp
from jax import lax
from jax.experimental import pallas as pl
from jax.experimental.pallas import tpu as pltpu
from jax.sharding import PartitionSpec as P

HD = 256
SPAN = 8
CORES = 2
CHIPS = SPAN // CORES
LOWEST = -1e29
NEG_FILL = -1e30
NORM_EPS = 1e-05
F32 = jnp.float32
BF16 = jnp.bfloat16


def swap_cores(value):
    pairs = [(k, k ^ 1) for k in range(lax.axis_size("kv"))]
    return lax.ppermute(value, "kv", pairs)


def next_chip(value):
    pairs = [
        (k, k - k % SPAN + (k % SPAN + CORES) % SPAN) for k in range(lax.axis_size("kv"))
    ]
    return lax.ppermute(value, "kv", pairs)


def widen(pieces, bit):
    device_count = lax.axis_size("kv") * lax.axis_size("req")
    pairs = [(d, d ^ (SPAN << bit)) for d in range(device_count)]
    found = dict(pieces)
    for index, piece in pieces.items():
        found[index | 1 << bit] = lax.ppermute(piece, ("req", "kv"), pairs)
    return found


def gather_in_order(value):
    size = lax.axis_size("kv")
    if size > SPAN:
        groups = [list(range(m, size, SPAN)) for m in range(SPAN)]
        value = lax.all_gather(value, "kv", axis=0, tiled=True, axis_index_groups=groups)
    return lax.all_gather(value, "req", axis=0, tiled=True)


def layer_norm(stream, norm_gain):
    values = stream.astype(F32)
    centred = values - jnp.mean(values, axis=-1, keepdims=True)
    spread = jnp.mean(centred * centred, axis=-1, keepdims=True)
    return (centred * lax.rsqrt(spread + NORM_EPS) * norm_gain).astype(BF16)


def attend_kernel(meta, *refs):
    pieces = refs[: 2 * CHIPS]
    key, value, new_key, new_value, bias, out, lse, value_t, new_value_t = refs[2 * CHIPS :]
    slot = pl.program_id(0)
    core = meta[2]
    member = meta[3]
    chip = member // CORES
    token_count = new_key.shape[0]
    half = CHIPS * token_count
    value_t[...] = value[...].T
    new_value_t[...] = new_value[...].T
    position = member * token_count + lax.broadcasted_iota(jnp.int32, (token_count, 1), 0)
    lane = lax.broadcasted_iota(jnp.int32, (1, token_count), 1)
    for first in (0, 1):
        source_core = core if first == 0 else 1 - core
        place = jnp.where(slot == 0, first, 1 - first) * half
        for pair in range(0, CHIPS, 2):
            steps = (pair, pair + 1)
            chips = [lax.rem(chip - step + CHIPS, CHIPS) for step in steps]
            queries = jnp.concatenate(
                [pieces[first * CHIPS + step][...] for step in steps], 0
            ) * BF16(HD**-0.5)
            scores = lax.dot_general(
                key[...], queries, (((1,), (1,)), ((), ())), preferred_element_type=F32
            )
            scores = scores + bias[...]
            fresh = lax.dot_general(
                new_key[...], queries, (((1,), (1,)), ((), ())), preferred_element_type=F32
            )
            token = jnp.concatenate(
                [(CORES * place_z + source_core) * token_count + lane for place_z in chips], 1
            )
            fresh = jnp.where(position <= token, fresh, NEG_FILL)
            largest = jnp.maximum(
                jnp.max(scores, axis=0, keepdims=True), jnp.max(fresh, axis=0, keepdims=True)
            )
            largest = jnp.maximum(largest, LOWEST)
            weights = jnp.exp(scores - largest)
            fresh = jnp.exp(fresh - largest)
            total = jnp.sum(weights, axis=0, keepdims=True) + jnp.sum(
                fresh, axis=0, keepdims=True
            )
            total = jnp.maximum(total, 1.0)
            sums = jnp.dot(
                value_t[...], weights.astype(BF16), preferred_element_type=F32
            ) + jnp.dot(new_value_t[...], fresh.astype(BF16), preferred_element_type=F32)
            sums = (sums / total).astype(BF16)
            logs = largest + jnp.log(total)
            for step, place_z in enumerate(chips):
                lanes = pl.ds(
                    pl.multiple_of(place + place_z * token_count, token_count), token_count
                )
                held = slice(step * token_count, (step + 1) * token_count)
                out[0, :, lanes] = sums[:, held]
                lse[0, :, lanes] = logs[:, held]


def attend(meta, pieces, key_cache, value_cache, projections, bias):
    token_count = projections.shape[0]
    new_total = len(pieces) * token_count
    cache_rows = key_cache.shape[0]
    heads = key_cache.shape[1] // HD
    q_spec = pl.BlockSpec((token_count, HD), lambda i, meta: (0, meta[i]))
    cache_spec = pl.BlockSpec((cache_rows, HD), lambda i, meta: (0, meta[i]))
    flops = 2 * 2 * CORES * new_total * (cache_rows + token_count) * HD
    return pl.pallas_call(
        attend_kernel,
        grid_spec=pltpu.PrefetchScalarGridSpec(
            num_scalar_prefetch=1,
            grid=(CORES,),
            in_specs=[q_spec] * len(pieces)
            + [
                cache_spec,
                cache_spec,
                pl.BlockSpec((token_count, HD), lambda i, meta: (0, heads + meta[i])),
                pl.BlockSpec((token_count, HD), lambda i, meta: (0, 2 * heads + meta[i])),
                pl.BlockSpec((cache_rows, 1), lambda i, meta: (0, 0)),
            ],
            out_specs=[
                pl.BlockSpec((1, HD, new_total), lambda i, meta: (i, 0, 0)),
                pl.BlockSpec((1, 1, new_total), lambda i, meta: (i, 0, 0)),
            ],
            scratch_shapes=[
                pltpu.VMEM((HD, cache_rows), BF16),
                pltpu.VMEM((HD, token_count), BF16),
            ],
        ),
        out_shape=[
            jax.ShapeDtypeStruct((CORES, HD, new_total), BF16),
            jax.ShapeDtypeStruct((CORES, 1, new_total), F32),
        ],
        compiler_params=pltpu.CompilerParams(vmem_limit_bytes=40 * 2**20),
        cost_estimate=pl.CostEstimate(
            flops=flops, bytes_accessed=8 * 2**20, transcendentals=flops // (4 * HD)
        ),
    )(meta, *pieces, key_cache, value_cache, projections, projections, bias)


def units_kernel(rows, up, down, out):
    unit_count = up.shape[0]
    block = min(256, unit_count)
    total = jnp.zeros(out.shape, F32)
    for first in range(0, unit_count, block):
        gates = lax.dot_general(
            rows[...],
            up[first : first + block, :],
            (((1,), (1,)), ((), ())),
            preferred_element_type=F32,
        )
        hidden = (gates * 0.5 * (1.0 + lax.erf(gates * (0.5**0.5)))).astype(BF16)
        total = total + jnp.dot(
            hidden, down[first : first + block, :], preferred_element_type=F32
        )
    out[...] = total


def all_units(rows, up_rows, down_rows):
    row_count, width = rows.shape
    unit_count = up_rows.shape[0]
    block = min(256, row_count)
    weights = pl.BlockSpec((unit_count, width), lambda i: (0, 0), pipeline_mode=pl.Buffered(1))
    rows_spec = pl.BlockSpec((block, width), lambda i: (i, 0))
    return pl.pallas_call(
        units_kernel,
        grid=(row_count // block,),
        in_specs=[rows_spec, weights, weights],
        out_specs=rows_spec,
        out_shape=jax.ShapeDtypeStruct((row_count, width), F32),
        compiler_params=pltpu.CompilerParams(vmem_limit_bytes=40 * 2**20),
        cost_estimate=pl.CostEstimate(
            flops=4 * row_count * width * unit_count,
            bytes_accessed=20 * 2**20,
            transcendentals=row_count * unit_count,
        ),
    )(rows, up_rows, down_rows)


def merge(parts):
    largest = parts[0][1]
    for part in parts[1:]:
        largest = jnp.maximum(largest, part[1])
    shares = [jnp.exp(part[1] - largest) for part in parts]
    total = sum(shares)
    joined = sum(part[0].astype(F32) * (share / total) for part, share in zip(parts, shares))
    return joined.astype(BF16), largest + jnp.log(total)


def on_device(
    stream,
    projections,
    key_cache,
    value_cache,
    cache_range,
    norm_gain,
    out_weight,
    up_weight,
    down_weight,
):
    token_count, width = stream.shape
    cache_rows = key_cache.shape[0]
    kv_count = lax.axis_size("kv")
    device_count = kv_count * lax.axis_size("req")
    request_count = device_count // SPAN
    kv_place = lax.axis_index("kv")
    member = kv_place % SPAN
    core = member % CORES
    chip = member // CORES
    request = (lax.axis_index("req") * kv_count + kv_place) // SPAN

    bits = list(range(request_count.bit_length() - 1))
    q_mine = [projections[:, :width]]
    up_pieces, down_pieces = {0: up_weight}, {0: down_weight}
    for step in range(CHIPS - 2):
        q_mine.append(next_chip(q_mine[-1]))
    up_pieces = widen(up_pieces, bits[0])
    down_pieces = widen(down_pieces, bits[-1])
    q_other = [swap_cores(piece) for piece in q_mine[:-1]]
    q_mine[-1], q_other, up_pieces, down_pieces = lax.optimization_barrier(
        (q_mine[-1], q_other, up_pieces, down_pieces)
    )
    q_mine.append(next_chip(q_mine[-1]))
    q_other += [swap_cores(piece) for piece in q_mine[-2:]]
    for bit in bits[1:]:
        up_pieces = widen(up_pieces, bit)
    for bit in reversed(bits[:-1]):
        down_pieces = widen(down_pieces, bit)
    head_pairs = [
        (d, (d % request_count) * SPAN + d // request_count) for d in range(device_count)
    ]
    out_rows = gather_in_order(lax.ppermute(out_weight, ("req", "kv"), head_pairs))

    bounds = lax.dynamic_slice_in_dim(cache_range, request, 1, 0)[0]
    positions = member * cache_rows + jnp.arange(cache_rows, dtype=jnp.int32)[:, None]
    bias = jnp.where((positions >= bounds[0]) & (positions < bounds[1]), 0.0, NEG_FILL)
    bias = bias.astype(F32)

    normed, _ = lax.optimization_barrier((layer_norm(stream, norm_gain), q_mine[-1]))
    rows_mine = [normed, next_chip(normed)]
    rows_other = [swap_cores(normed)]

    carried = None
    for phase in range(CHIPS):
        target = (chip + CHIPS - 1 - phase) % CHIPS
        kept = CORES * target + core
        given = CORES * target + 1 - core
        meta = jnp.stack([kept, given, core, member]).astype(jnp.int32)
        if phase % 2 == 1:
            meta, rows_mine, rows_other = lax.optimization_barrier((meta, rows_mine, rows_other))
            rows_mine.append(next_chip(rows_mine[-1]))
            rows_other.append(swap_cores(rows_mine[-2]))
        out, lse = attend(meta, q_mine + q_other, key_cache, value_cache, projections, bias)
        if phase == CHIPS - 2:
            out, up_pieces, down_pieces = lax.optimization_barrier((out, up_pieces, down_pieces))
        parts = [(out[0], lse[0]), swap_cores((out[1], lse[1]))]
        if carried is not None:
            parts.append(carried)
        carried = merge(parts)
        if phase < CHIPS - 1:
            carried = next_chip(carried)
    up_rows = jnp.concatenate([up_pieces[i] for i in range(request_count)], 0)
    down_rows = jnp.concatenate([down_pieces[i] for i in range(request_count)], 0)
    rows_other += [swap_cores(piece) for piece in rows_mine[len(rows_other) :]]
    rows = jnp.concatenate(rows_mine + rows_other, 0)
    units = all_units(rows, up_rows, down_rows)
    attention, units = lax.optimization_barrier((carried[0], units))

    half = CHIPS * token_count
    order = [(step + 1) % CHIPS for step in range(CHIPS)]
    firsts = [((chip + CHIPS - step) % CHIPS) * token_count for step in order]

    def branch(offset):
        block = jnp.concatenate(
            [
                lax.dynamic_slice_in_dim(attention, offset + first, token_count, 1)
                for first in firsts
            ],
            1,
        )
        return lax.dot_general(
            block, out_rows, (((0,), (0,)), ((), ())), preferred_element_type=F32
        )

    def units_of(offset, step):
        first = offset + step * token_count
        return units[first : first + token_count]

    given, kept = branch(half), branch(0)
    received = []
    for phase, step in enumerate(order):
        rows = slice(phase * token_count, (phase + 1) * token_count)
        received.append(swap_cores((given[rows] + units_of(half, step)).astype(BF16)))
    running = None
    for phase, step in enumerate(order):
        rows = slice(phase * token_count, (phase + 1) * token_count)
        total = kept[rows] + units_of(0, step) + received[phase].astype(F32)
        if running is not None:
            total = total + running.astype(F32)
        running = total
        if phase < CHIPS - 1:
            running = next_chip(total.astype(BF16))
    return (stream.astype(F32) + running).astype(BF16)


def solution(mesh):
    rows = P(("req", "kv"), None)
    in_specs = (rows, rows, rows, rows, P(), P(), rows, rows, rows)
    return jax.shard_map(
        on_device, mesh=mesh, in_specs=in_specs, out_specs=rows, check_vma=False
    )
```

```python
import jax
import jax.numpy as jnp
from jax import lax
from jax.experimental import pallas as pl
from jax.experimental.pallas import tpu as pltpu
from jax.sharding import PartitionSpec as P

HD = 256
SPAN = 8
CORES = 2
CHIPS = SPAN // CORES
LOWEST = -1e29
NEG_FILL = -1e30
NORM_EPS = 1e-05
F32 = jnp.float32
BF16 = jnp.bfloat16


def swap_cores(value):
    pairs = [(k, k ^ 1) for k in range(lax.axis_size("kv"))]
    return lax.ppermute(value, "kv", pairs)


def next_chip(value):
    pairs = [
        (k, k - k % SPAN + (k % SPAN + CORES) % SPAN) for k in range(lax.axis_size("kv"))
    ]
    return lax.ppermute(value, "kv", pairs)


def widen(rows, bit):
    device_count = lax.axis_size("kv") * lax.axis_size("req")
    pairs = [(d, d ^ (SPAN << bit)) for d in range(device_count)]
    return jnp.concatenate([rows, lax.ppermute(rows, ("req", "kv"), pairs)], 0)


def gather_in_order(value):
    size = lax.axis_size("kv")
    if size > SPAN:
        groups = [list(range(m, size, SPAN)) for m in range(SPAN)]
        value = lax.all_gather(value, "kv", axis=0, tiled=True, axis_index_groups=groups)
    return lax.all_gather(value, "req", axis=0, tiled=True)


def layer_norm(stream, norm_gain):
    values = stream.astype(F32)
    centred = values - jnp.mean(values, axis=-1, keepdims=True)
    spread = jnp.mean(centred * centred, axis=-1, keepdims=True)
    return (centred * lax.rsqrt(spread + NORM_EPS) * norm_gain).astype(BF16)


def attend_kernel(meta, *refs):
    pieces = refs[: 2 * CHIPS]
    key, value, new_key, new_value, bias, out, lse, value_t, new_value_t = refs[2 * CHIPS :]
    slot = pl.program_id(0)
    core = meta[2]
    member = meta[3]
    chip = member // CORES
    token_count = new_key.shape[0]
    half = CHIPS * token_count
    value_t[...] = value[...].T
    new_value_t[...] = new_value[...].T
    position = member * token_count + lax.broadcasted_iota(jnp.int32, (token_count, 1), 0)
    lane = lax.broadcasted_iota(jnp.int32, (1, token_count), 1)
    for first in (0, 1):
        source_core = core if first == 0 else 1 - core
        place = jnp.where(slot == 0, first, 1 - first) * half
        for pair in range(0, CHIPS, 2):
            steps = (pair, pair + 1)
            chips = [lax.rem(chip - step + CHIPS, CHIPS) for step in steps]
            queries = jnp.concatenate(
                [pieces[first * CHIPS + step][...] for step in steps], 0
            ) * BF16(HD**-0.5)
            scores = lax.dot_general(
                key[...], queries, (((1,), (1,)), ((), ())), preferred_element_type=F32
            )
            scores = scores + bias[...]
            fresh = lax.dot_general(
                new_key[...], queries, (((1,), (1,)), ((), ())), preferred_element_type=F32
            )
            token = jnp.concatenate(
                [(CORES * place_z + source_core) * token_count + lane for place_z in chips], 1
            )
            fresh = jnp.where(position <= token, fresh, NEG_FILL)
            largest = jnp.maximum(
                jnp.max(scores, axis=0, keepdims=True), jnp.max(fresh, axis=0, keepdims=True)
            )
            largest = jnp.maximum(largest, LOWEST)
            weights = jnp.exp(scores - largest)
            fresh = jnp.exp(fresh - largest)
            total = jnp.sum(weights, axis=0, keepdims=True) + jnp.sum(
                fresh, axis=0, keepdims=True
            )
            total = jnp.maximum(total, 1.0)
            sums = jnp.dot(
                value_t[...], weights.astype(BF16), preferred_element_type=F32
            ) + jnp.dot(new_value_t[...], fresh.astype(BF16), preferred_element_type=F32)
            sums = (sums / total).astype(BF16)
            logs = largest + jnp.log(total)
            for step, place_z in enumerate(chips):
                lanes = pl.ds(
                    pl.multiple_of(place + place_z * token_count, token_count), token_count
                )
                held = slice(step * token_count, (step + 1) * token_count)
                out[0, :, lanes] = sums[:, held]
                lse[0, :, lanes] = logs[:, held]


def attend(meta, pieces, key_cache, value_cache, projections, bias):
    token_count = projections.shape[0]
    new_total = len(pieces) * token_count
    cache_rows = key_cache.shape[0]
    heads = key_cache.shape[1] // HD
    q_spec = pl.BlockSpec((token_count, HD), lambda i, meta: (0, meta[i]))
    cache_spec = pl.BlockSpec((cache_rows, HD), lambda i, meta: (0, meta[i]))
    flops = 2 * 2 * CORES * new_total * (cache_rows + token_count) * HD
    return pl.pallas_call(
        attend_kernel,
        grid_spec=pltpu.PrefetchScalarGridSpec(
            num_scalar_prefetch=1,
            grid=(CORES,),
            in_specs=[q_spec] * len(pieces)
            + [
                cache_spec,
                cache_spec,
                pl.BlockSpec((token_count, HD), lambda i, meta: (0, heads + meta[i])),
                pl.BlockSpec((token_count, HD), lambda i, meta: (0, 2 * heads + meta[i])),
                pl.BlockSpec((cache_rows, 1), lambda i, meta: (0, 0)),
            ],
            out_specs=[
                pl.BlockSpec((1, HD, new_total), lambda i, meta: (i, 0, 0)),
                pl.BlockSpec((1, 1, new_total), lambda i, meta: (i, 0, 0)),
            ],
            scratch_shapes=[
                pltpu.VMEM((HD, cache_rows), BF16),
                pltpu.VMEM((HD, token_count), BF16),
            ],
        ),
        out_shape=[
            jax.ShapeDtypeStruct((CORES, HD, new_total), BF16),
            jax.ShapeDtypeStruct((CORES, 1, new_total), F32),
        ],
        compiler_params=pltpu.CompilerParams(vmem_limit_bytes=40 * 2**20),
        cost_estimate=pl.CostEstimate(
            flops=flops, bytes_accessed=8 * 2**20, transcendentals=flops // (4 * HD)
        ),
    )(meta, *pieces, key_cache, value_cache, projections, projections, bias)


def units_kernel(rows, up, down, out):
    unit_count = up.shape[0]
    block = min(256, unit_count)
    total = jnp.zeros(out.shape, F32)
    for first in range(0, unit_count, block):
        gates = lax.dot_general(
            rows[...],
            up[first : first + block, :],
            (((1,), (1,)), ((), ())),
            preferred_element_type=F32,
        )
        hidden = (gates * 0.5 * (1.0 + lax.erf(gates * (0.5**0.5)))).astype(BF16)
        total = total + jnp.dot(
            hidden, down[first : first + block, :], preferred_element_type=F32
        )
    out[...] = total


def all_units(rows, up_rows, down_rows):
    row_count, width = rows.shape
    unit_count = up_rows.shape[0]
    block = min(256, row_count)
    weights = pl.BlockSpec((unit_count, width), lambda i: (0, 0), pipeline_mode=pl.Buffered(1))
    rows_spec = pl.BlockSpec((block, width), lambda i: (i, 0))
    return pl.pallas_call(
        units_kernel,
        grid=(row_count // block,),
        in_specs=[rows_spec, weights, weights],
        out_specs=rows_spec,
        out_shape=jax.ShapeDtypeStruct((row_count, width), F32),
        compiler_params=pltpu.CompilerParams(vmem_limit_bytes=40 * 2**20),
        cost_estimate=pl.CostEstimate(
            flops=4 * row_count * width * unit_count,
            bytes_accessed=20 * 2**20,
            transcendentals=row_count * unit_count,
        ),
    )(rows, up_rows, down_rows)


def merge(parts):
    largest = parts[0][1]
    for part in parts[1:]:
        largest = jnp.maximum(largest, part[1])
    shares = [jnp.exp(part[1] - largest) for part in parts]
    total = sum(shares)
    joined = sum(part[0].astype(F32) * (share / total) for part, share in zip(parts, shares))
    return joined.astype(BF16), largest + jnp.log(total)


def on_device(
    stream,
    projections,
    key_cache,
    value_cache,
    cache_range,
    norm_gain,
    out_weight,
    up_weight,
    down_weight,
):
    token_count, width = stream.shape
    cache_rows = key_cache.shape[0]
    kv_count = lax.axis_size("kv")
    device_count = kv_count * lax.axis_size("req")
    request_count = device_count // SPAN
    kv_place = lax.axis_index("kv")
    member = kv_place % SPAN
    core = member % CORES
    chip = member // CORES
    request = (lax.axis_index("req") * kv_count + kv_place) // SPAN

    bits = list(range(request_count.bit_length() - 1))
    q_mine = [projections[:, :width]]
    for step in range(CHIPS - 2):
        q_mine.append(next_chip(q_mine[-1]))
    up_rows = widen(up_weight, bits[0])
    down_rows = widen(down_weight, bits[-1])
    q_other = [swap_cores(piece) for piece in q_mine[:-1]]
    q_mine[-1], q_other, up_rows, down_rows = lax.optimization_barrier(
        (q_mine[-1], q_other, up_rows, down_rows)
    )
    q_mine.append(next_chip(q_mine[-1]))
    q_other += [swap_cores(piece) for piece in q_mine[-2:]]
    for bit in bits[1:]:
        up_rows = widen(up_rows, bit)
    for bit in reversed(bits[:-1]):
        down_rows = widen(down_rows, bit)
    head_pairs = [
        (d, (d % request_count) * SPAN + d // request_count) for d in range(device_count)
    ]
    out_rows = gather_in_order(lax.ppermute(out_weight, ("req", "kv"), head_pairs))

    bounds = lax.dynamic_slice_in_dim(cache_range, request, 1, 0)[0]
    positions = member * cache_rows + jnp.arange(cache_rows, dtype=jnp.int32)[:, None]
    bias = jnp.where((positions >= bounds[0]) & (positions < bounds[1]), 0.0, NEG_FILL)
    bias = bias.astype(F32)

    normed, _ = lax.optimization_barrier((layer_norm(stream, norm_gain), q_mine[-1]))
    rows_mine = [normed, next_chip(normed)]
    rows_other = [swap_cores(normed)]

    carried = None
    shares = []
    for phase in range(CHIPS):
        target = (chip + CHIPS - 1 - phase) % CHIPS
        kept = CORES * target + core
        given = CORES * target + 1 - core
        meta = jnp.stack([kept, given, core, member]).astype(jnp.int32)
        if phase % 2 == 1:
            meta, rows_mine, rows_other = lax.optimization_barrier((meta, rows_mine, rows_other))
            rows_mine.append(next_chip(rows_mine[-1]))
            rows_other.append(swap_cores(rows_mine[-2]))
        if phase == 2:
            meta, first = lax.optimization_barrier((meta, merge(shares[0])))
            carried = next_chip(first)
        if phase == 3:
            meta, shares[1] = lax.optimization_barrier((meta, shares[1]))
        out, lse = attend(meta, q_mine + q_other, key_cache, value_cache, projections, bias)
        shares.append([(out[0], lse[0]), swap_cores((out[1], lse[1]))])
    for phase in range(1, CHIPS):
        carried = merge(shares[phase] + [carried])
        if phase < CHIPS - 1:
            carried = next_chip(carried)
        if phase == 1:
            carried, up_rows, down_rows = lax.optimization_barrier(
                (carried, up_rows, down_rows)
            )
    unit_rows = down_weight.shape[0]
    down_rows = down_rows.reshape([2] * len(bits) + [unit_rows, width]).transpose(
        list(reversed(range(len(bits)))) + [len(bits), len(bits) + 1]
    )
    down_rows = down_rows.reshape(request_count * unit_rows, width)
    rows_other += [swap_cores(piece) for piece in rows_mine[len(rows_other) :]]
    rows = jnp.concatenate(rows_mine + rows_other, 0)
    units = all_units(rows, up_rows, down_rows)
    attention, units = lax.optimization_barrier((carried[0], units))

    half = CHIPS * token_count
    order = [(step + 1) % CHIPS for step in range(CHIPS)]
    firsts = [((chip + CHIPS - step) % CHIPS) * token_count for step in order]

    def branch(offset):
        block = jnp.concatenate(
            [
                lax.dynamic_slice_in_dim(attention, offset + first, token_count, 1)
                for first in firsts
            ],
            1,
        )
        return lax.dot_general(
            block, out_rows, (((0,), (0,)), ((), ())), preferred_element_type=F32
        )

    def units_of(offset, step):
        first = offset + step * token_count
        return units[first : first + token_count]

    given, kept = branch(half), branch(0)
    received = []
    for phase, step in enumerate(order):
        rows = slice(phase * token_count, (phase + 1) * token_count)
        received.append(swap_cores((given[rows] + units_of(half, step)).astype(BF16)))
    running = None
    for phase, step in enumerate(order):
        rows = slice(phase * token_count, (phase + 1) * token_count)
        total = kept[rows] + units_of(0, step) + received[phase].astype(F32)
        if running is not None:
            total = total + running.astype(F32)
        running = total
        if phase < CHIPS - 1:
            running = next_chip(total.astype(BF16))
    return (stream.astype(F32) + running).astype(BF16)


def solution(mesh):
    rows = P(("req", "kv"), None)
    in_specs = (rows, rows, rows, rows, P(), P(), rows, rows, rows)
    return jax.shard_map(
        on_device, mesh=mesh, in_specs=in_specs, out_specs=rows, check_vma=False
    )
```
